128 devices in a mesh: tm: 32 (over y_lo, z, x), freq: 4 (over y_hi, core).
Axes of the slice: x: 4, y: 4 (y_hi: 2, y_lo: 2; y = y_hi * 2 + y_lo), z: 4, core: 2. Of those that a mesh axis runs over, the one named last changes fastest.
Arguments:
- waveform: float32 [4194304], P(('tm', 'freq')), may hold values from -24.5 to 24.5
- starts: int32 [16384], P(('tm', 'freq')), may hold values from 0 to 4194303, as said below
- templates: float32 [1024, 512], P('freq'), may hold values from 0.05 to 2
- activations: float32 [16384, 512], P('tm', 'freq'), may hold values from 0.05 to 2
Outputs:
- templates_out: float32 [1024, 512], P('freq')
- activations_out: float32 [16384, 512], P('tm', 'freq')
The draws below stay inside these ranges and needn't reach their ends.
Inputs may be any that keep to these rules, and one draw needn't show every extreme that they name: Frame j starts within the stretch of 32768 samples numbered j // 128: (j // 128) * 32768 <= starts[j] < (j // 128 + 1) * 32768.
All inputs are finite; a program needn't handle non-finite values.
Results may differ from the reference program's by a relative error of at most 0.003.
The reference program's roundings to bfloat16 on the way (of `frames`, `fourier` and `ratios`) count: a program that leaves them out, or rounds other values in their place, can miss the bound.
Values may be sent and summed in bfloat16 or wider, within the bound.
A program may use at most 64 MiB of HBM per device.

```python
import math
import jax
import jax.numpy as jnp
from jax import lax

FLEN = 2048
BINS = 1024
K = 512
ITERS = 2
FR_DEV = 128
SEG = 32768
FRAMES = 16384
SAMPLES = 4194304


def draw_starts(key, part):
    block_count = FRAMES // FR_DEV
    inside_starts = jax.random.randint(jax.random.fold_in(key, 11), (block_count, FR_DEV), 0, SEG)
    edge_starts = jax.random.randint(jax.random.fold_in(key, 12), (block_count, 1), SEG - FLEN + 1, SEG)
    edge_column = jax.random.randint(jax.random.fold_in(key, 13), (block_count, 1), 0, FR_DEV)
    chosen = jnp.where(jnp.arange(FR_DEV)[None, :] == edge_column, edge_starts, inside_starts)
    return (chosen + jnp.arange(block_count)[:, None] * SEG).reshape(FRAMES).astype(jnp.int32)


def draw_waveform(key, part):
    spacing = FLEN // 4
    blocks = SAMPLES // spacing + 1
    place = jax.random.randint(jax.random.fold_in(key, 21), (blocks,), 0, spacing)
    sign_bits = jax.random.randint(jax.random.fold_in(key, 22), (blocks,), 0, 2)
    signs = sign_bits.astype(jnp.float32) * 2.0 - 1.0
    magnitude = jax.random.uniform(jax.random.fold_in(key, 23), (blocks,), jnp.float32, 8.0, 24.0)
    background = jnp.clip(0.05 * jax.random.normal(jax.random.fold_in(key, 24), (blocks * spacing,), jnp.float32), -0.25, 0.25)
    spikes = jnp.where(jnp.arange(spacing)[None, :] == place[:, None], (signs * magnitude)[:, None], 0.0)
    return (spikes.reshape(-1) + background)[:SAMPLES].astype(jnp.float32)


def block_scale(stream_key, dims, shards, low, largest):
    def one(position, blocks):
        steps = jax.random.uniform(jax.random.fold_in(jax.random.fold_in(stream_key, 6), position), (blocks,), jnp.float32, low / len(shards), largest / len(shards))
        return jnp.repeat(jnp.exp(steps), dims[position] // blocks).reshape((-1,) + (1,) * (len(dims) - position - 1))

    gain = one(*shards[0])
    for cut in shards[1:]:
        gain = gain * one(*cut)
    return gain


def setup_inputs(seed: int = 0) -> dict:
    splits = jax.random.split(jax.random.key(seed), 5)
    waveform = draw_waveform(jax.random.fold_in(splits[4], 71), 0)
    starts = draw_starts(jax.random.fold_in(splits[4], 71), 0)
    templates = jnp.clip(jnp.exp(math.log(2.0) - 3.6888794 * jax.random.uniform(splits[2], (BINS, K), jnp.float32) ** block_scale(splits[2], (BINS, K), ((0, 4),), -0.2, 0.2)), 0.05, 2.0)
    activations = jnp.clip(jnp.exp(math.log(2.0) - 3.6888794 * jax.random.uniform(splits[3], (FRAMES, K), jnp.float32) ** block_scale(splits[3], (FRAMES, K), ((0, 32), (1, 4)), -0.2, 0.2)), 0.05, 2.0)
    return {"waveform": waveform, "starts": starts, "templates": templates, "activations": activations}


def fourier_table(length, bins):
    row_index = jnp.arange(length, dtype=jnp.int32)[:, None]
    bin_index = jnp.arange(bins, dtype=jnp.int32)[None, :]
    phase = ((row_index * bin_index) % length).astype(jnp.float32) * (2.0 * math.pi / length)
    return jnp.concatenate([jnp.cos(phase), -jnp.sin(phase)], axis=1).astype(jnp.bfloat16)


def hann_window(length):
    steps_all = jnp.arange(length, dtype=jnp.int32).astype(jnp.float32)
    return 0.5 - 0.5 * jnp.cos(steps_all * (2.0 * math.pi / length))


def reference(waveform, starts, templates, activations):
    fourier = fourier_table(FLEN, BINS)
    window = hann_window(FLEN)
    padded = jnp.concatenate([waveform, jnp.zeros((FLEN,), waveform.dtype)])

    def one_block(block_starts):
        frames = jax.vmap(lambda offset: lax.dynamic_slice(padded, (offset,), (FLEN,)))(block_starts)
        frames = (frames * window[None, :]).astype(jnp.bfloat16)
        spectrum = jnp.dot(frames, fourier, preferred_element_type=jnp.float32)
        return (spectrum[:, :BINS] ** 2 + spectrum[:, BINS:] ** 2) * 0.25

    energy = lax.map(one_block, starts.reshape(-1, FR_DEV)).reshape(FRAMES, BINS)
    weights_now = templates
    acts_now = activations
    for iteration in range(ITERS):
        templates_half = weights_now.astype(jnp.bfloat16)
        acts_half = acts_now.astype(jnp.bfloat16)
        rebuilt = lax.dot_general(acts_half, templates_half, (((1,), (1,)), ((), ())), preferred_element_type=jnp.float32)
        ratios = (energy / rebuilt).astype(jnp.bfloat16)
        numerator = jnp.dot(ratios, templates_half, preferred_element_type=jnp.float32)
        template_mass = jnp.sum(weights_now, axis=0)
        acts_now = acts_now * numerator / template_mass[None, :]
        acts_half = acts_now.astype(jnp.bfloat16)
        rebuilt = lax.dot_general(acts_half, templates_half, (((1,), (1,)), ((), ())), preferred_element_type=jnp.float32)
        ratios = (energy / rebuilt).astype(jnp.bfloat16)
        template_numerator = lax.dot_general(ratios, acts_half, (((0,), (0,)), ((), ())), preferred_element_type=jnp.float32)
        column_totals = jnp.sum(acts_half.astype(jnp.float32), axis=0)
        weights_now = weights_now * template_numerator / column_totals[None, :]
    return weights_now, acts_now
```

```python
import jax
import jax.numpy as jnp
import numpy as np
from jax import lax
from jax.experimental import pallas as pl
from jax.experimental.pallas import tpu as pltpu
from jax.sharding import PartitionSpec as P

FLEN = 2048
BINS = 1024
K = 512
ITERS = 2
SEG = 32768
FR = 128
GROUPS = 4
MESH = pl.DeviceIdType.MESH
F32 = jnp.float32
BF16 = jnp.bfloat16


def half_tables():
    row = np.arange(FLEN, dtype=np.int64)[:, None]
    tables = []
    for core in range(2):
        bins = np.concatenate([np.arange(256) + 256 * core, np.arange(256) + 512 + 256 * core])
        phase = ((row * bins[None, :]) % FLEN).astype(np.float32) * np.float32(2.0 * np.pi / FLEN)
        tables.append(np.concatenate([np.cos(phase), -np.sin(phase)], axis=1))
    return np.stack(tables).astype(jnp.bfloat16)


def hann_window():
    steps = np.arange(FLEN, dtype=np.float32) * np.float32(2.0 * np.pi / FLEN)
    return (np.float32(0.5) - np.float32(0.5) * np.cos(steps)).reshape(16, 128)


def hops(offset):
    return sum(min(v, 4 - v) for v in offset)


OFFSETS = sorted(
    [(dx, dy, dz) for dz in range(4) for dy in range(4) for dx in range(4) if dx or dy or dz],
    key=lambda offset: -hops(offset),
)


def dot(a, b, dims):
    return lax.dot_general(a, b, (dims, ((), ())), preferred_element_type=F32)


def kernel(
    wave_hbm, starts, window, table_hbm, templ_hbm, act_hbm, w_out, a_out,
    wave, table, templ, acts, gathered, frames, energy, energy_t, wb, own_w, w_last,
    part, part_got, t_send, t_got, tot, tot_got, mass, mass_half,
    local_sem, rim_sem, frame_send, frame_recv, act_send, act_recv, w_send, w_recv,
    part_send, part_recv, t_sems, mass_send, mass_recv, fin_sem, y_sem, z_sem,
):
    tm = lax.axis_index("tm")
    fr = lax.axis_index("freq")
    x, z, y_lo = lax.rem(tm, 4), lax.rem(lax.div(tm, 4), 4), lax.div(tm, 16)
    y_hi, core = lax.div(fr, 2), lax.rem(fr, 2)
    y = 2 * y_hi + y_lo
    xs = [lax.rem(x + d, 4) for d in range(4)]
    zs = [lax.rem(z + d, 4) for d in range(4)]
    ys = [lax.rem(y + d, 4) for d in range(4)]
    y_los = [lax.rem(v, 2) for v in ys]
    y_his = [lax.div(v, 2) for v in ys]

    def chip(dx, dy, dz):
        return (y_los[dy] * 16 + zs[dz] * 4 + xs[dx], y_his[dy] * 2 + core)

    def remote(src, dst, send, recv, device):
        return pltpu.make_async_remote_copy(
            src_ref=src, dst_ref=dst, send_sem=send, recv_sem=recv,
            device_id=device, device_id_type=MESH,
        )

    sibling = (tm, 2 * y_hi + 1 - core)
    across = (tm, 2 * (1 - y_hi) + core)
    beside = (lax.rem(tm + 16, 32), 2 * (1 - y_hi) + core)
    place = 4 * tm + fr
    following = lax.rem(place + 1, 128)
    previous = lax.rem(place + 127, 128)
    following = (lax.div(following, 4), lax.rem(following, 4))
    previous = (lax.div(previous, 4), lax.rem(previous, 4))

    copies = [
        pltpu.make_async_copy(wave_hbm, wave.at[pl.ds(0, 256)], local_sem.at[0]),
        pltpu.make_async_copy(act_hbm, acts.at[fr], local_sem.at[1]),
        pltpu.make_async_copy(templ_hbm, templ, local_sem.at[2]),
        pltpu.make_async_copy(table_hbm.at[core], table, local_sem.at[3]),
    ]
    barrier = pltpu.get_barrier_semaphore()
    axis_peers = [chip(d, 0, 0) for d in (1, 2, 3)]
    y_peers = [chip(0, d, 0) for d in (1, 2, 3)]
    z_peers = [chip(0, 0, d) for d in (1, 2, 3)]
    for device in [following, sibling] + axis_peers + y_peers + z_peers:
        pl.semaphore_signal(barrier, inc=1, device_id=device, device_id_type=MESH)
    for copy in copies:
        copy.start()
    copies[2].wait()
    for h in range(2):
        wb[h, pl.ds(16 * y_hi, 16)] = templ[:, 256 * h : 256 * h + 256].astype(BF16).reshape(16, 16, 256)
    mass[0, pl.ds(y_hi, 1)] = jnp.sum(templ[...], axis=0, keepdims=True).reshape(1, 1, K)
    g = 16 * y_hi + 4 * z + x
    for h in range(2):

        @pl.when(y_lo == h)
        def _():
            own_w[...] = templ[pl.ds(pl.multiple_of(16 * (4 * z + x), 16), 16), 256 * h : 256 * h + 256]

    copies[0].wait()
    copies[1].wait()
    pl.semaphore_wait(barrier, 11)

    rim = remote(wave.at[pl.ds(0, 16)], wave.at[pl.ds(256, 16)], rim_sem.at[0], rim_sem.at[1], previous)
    rim.start()
    here = pl.ds(pl.multiple_of(256 * y_hi, 256), 256)
    there = pl.ds(pl.multiple_of(256 * (1 - y_hi), 256), 256)
    act_across = remote(acts.at[fr, there], acts.at[fr, there], act_send.at[0], act_recv.at[0], across)
    act_across.start()
    act_sibling = remote(acts.at[fr, here], acts.at[fr, here], act_send.at[1], act_recv.at[1], sibling)
    act_sibling.start()
    w_copies = []
    for h in range(2):
        rows = wb.at[h, pl.ds(16 * y_hi, 16)]
        w_copies.append(remote(rows, rows, w_send.at[h], w_recv.at[h], beside))
    w_copies.append(remote(mass.at[0, y_hi], mass.at[0, y_hi], w_send.at[2], w_recv.at[2], beside))
    for copy in w_copies:
        copy.start()
    for device in y_peers:
        pl.semaphore_signal(y_sem, inc=1, device_id=device, device_id_type=MESH)

    rim.wait()

    @pl.when(place == 127)
    def _():
        wave[pl.ds(256, 16)] = jnp.zeros((16, 128), F32)

    lanes = lax.broadcasted_iota(jnp.int32, (16, 128), 1)
    scale = window[...]
    size = FR // GROUPS
    frame_copies = []
    for group in range(GROUPS):

        def gather(i, carry):
            start = lax.rem(starts[group * size + i], SEG)
            row, shift = lax.div(start, 128), lax.rem(start, 128)
            low = wave[pl.ds(row, 16), :]
            high = wave[pl.ds(row + 1, 16), :]
            joined = jnp.where(lanes >= shift, low, high)
            rolled = pltpu.roll(joined, lax.rem(128 - shift, 128), 1)
            gathered[pl.ds(i, 16, stride=size), :] = rolled * scale
            return carry

        lax.fori_loop(0, size, gather, 0, unroll=8)
        rows = pl.ds(pl.multiple_of(FR * core + group * size, size), size)
        for i in range(16):
            frames[rows, 128 * i : 128 * i + 128] = gathered[size * i : size * i + size, :].astype(BF16)
        copy = remote(frames.at[rows], frames.at[rows], frame_send.at[group], frame_recv.at[group], sibling)
        copy.start()
        frame_copies.append(copy)

    act_across.wait()
    far = 2 * (1 - y_hi) + core
    act_pass = remote(acts.at[far, here], acts.at[far, here], act_send.at[2], act_recv.at[2], sibling)
    act_pass.start()
    pl.semaphore_wait(y_sem, 3)
    for device in z_peers:
        pl.semaphore_signal(z_sem, inc=1, device_id=device, device_id_type=MESH)
    copies[3].wait()
    for copy in frame_copies:
        copy.wait()
    for j in range(2):
        cos = dot(frames[...], table[:, 256 * j : 256 * j + 256], ((1,), (0,)))
        sin = dot(frames[...], table[:, 512 + 256 * j : 768 + 256 * j], ((1,), (0,)))
        square = (cos * cos + sin * sin) * 0.25
        energy[:, 256 * j : 256 * j + 256] = square
        energy_t[256 * j : 256 * j + 256, :] = square.T
    for copy in w_copies:
        copy.wait()
    act_sibling.wait()
    act_pass.wait()
    pl.semaphore_wait(z_sem, 3)

    for t in range(ITERS):
        w_half = [wb[h].reshape(512, 256) for h in range(2)]
        if t == 0:
            half = mass[0, 0] + mass[0, 1]
        else:
            half = jnp.concatenate(
                [jnp.sum(w.astype(F32), axis=0, keepdims=True) for w in w_half], axis=1
            )
        mass_half[t, 0] = half
        mass_copy = remote(mass_half.at[t, 0], mass_half.at[t, 1], mass_send.at[t], mass_recv.at[t], sibling)
        mass_copy.start()
        hb = [acts[f, here].astype(BF16) for f in range(4)]
        hb = [jnp.concatenate(hb[:2], axis=1), jnp.concatenate(hb[2:], axis=1)]
        rebuilt = dot(hb[0], w_half[0], ((1,), (1,))) + dot(hb[1], w_half[1], ((1,), (1,)))
        ratios = (energy[...] / rebuilt).astype(BF16)
        part_copies = []
        for h in range(2):
            part[t, h] = dot(ratios, w_half[h], ((1,), (0,)))
            copy = remote(part.at[t, h], part_got.at[t, h], part_send.at[t, h], part_recv.at[t, h], sibling)
            copy.start()
            part_copies.append(copy)
        mass_copy.wait()
        inverse = 1.0 / (mass_half[t, 0] + mass_half[t, 1])
        hb = []
        for h in range(2):
            part_copies[h].wait()
            factor = (part[t, h] + part_got[t, h]) * inverse[:, 256 * h : 256 * h + 256]
            pieces = []
            for k in range(2):
                new = acts[2 * h + k, here] * factor[:, 128 * k : 128 * k + 128]
                acts[2 * h + k, here] = new
                pieces.append(new.astype(BF16))
            hb.append(jnp.concatenate(pieces, axis=1))
            tot[t, h] = jnp.sum(hb[h].astype(F32), axis=0, keepdims=True)
        if t == ITERS - 1:
            final = remote(acts.at[far, here], acts.at[far, here], fin_sem.at[0], fin_sem.at[1], across)
            final.start()

        rebuilt = dot(w_half[0], hb[0], ((1,), (1,))) + dot(w_half[1], hb[1], ((1,), (1,)))
        ratios = (energy_t[...] / rebuilt).astype(BF16)
        for h in range(2):
            t_send[h] = dot(ratios, hb[h], ((1,), (0,))).astype(BF16).reshape(32, 16, 256)
        for slot, (dx, dy, dz) in enumerate(OFFSETS):
            owner = 16 * y_his[dy] + 4 * zs[dz] + xs[dx]
            remote(
                t_send.at[y_los[dy], owner], t_got.at[slot], t_sems.at[0], t_sems.at[1], chip(dx, dy, dz)
            ).start()
            remote(
                tot.at[t, y_los[dy]], tot_got.at[slot], t_sems.at[2], t_sems.at[3], chip(dx, dy, dz)
            ).start()
        total = tot[t, y_lo]
        summed = t_send[y_lo, g].astype(F32)
        for s in (2, 3):
            pltpu.make_async_copy(tot_got, tot_got, t_sems.at[s]).wait()
        for s in (0, 1):
            pltpu.make_async_copy(t_got, t_got, t_sems.at[s]).wait()
        total = total + jnp.sum(tot_got[...], axis=0)
        summed = summed + jnp.sum(t_got[...].astype(F32), axis=0)
        new_w = own_w[...] * summed / total
        if t < ITERS - 1:
            own_w[...] = new_w
            wb[y_lo, g] = new_w.astype(BF16)
            for dx, dy, dz in OFFSETS:
                remote(
                    wb.at[y_lo, g], wb.at[y_lo, g], t_sems.at[4], t_sems.at[5], chip(dx, dy, dz)
                ).start()
            for s in (4, 5):
                pltpu.make_async_copy(t_got, t_got, t_sems.at[s]).wait()
        else:
            w_last[y_lo, 4 * z + x] = new_w.astype(BF16)
            count = 0
            for dx, dy, dz in OFFSETS:
                if dy > 1:
                    continue
                other = 1 - y_lo if dy else y_lo
                device = (16 * other + 4 * zs[dz] + xs[dx], fr)
                mine = w_last.at[y_lo, 4 * z + x]
                remote(mine, mine, t_sems.at[6], t_sems.at[7], device).start()
                count += 1
            a_out[here, :] = acts[fr, here]
            final.wait()
            a_out[there, :] = acts[fr, there]
            waited = t_got.at[pl.ds(0, count)]
            for s in (6, 7):
                pltpu.make_async_copy(waited, waited, t_sems.at[s]).wait()
            for h in range(2):
                w_out[:, 256 * h : 256 * h + 256] = w_last[h].reshape(256, 256).astype(F32)


def shards(waveform, starts, templates, activations):
    hbm = pl.BlockSpec(memory_space=pl.ANY)
    vmem = pl.BlockSpec(memory_space=pltpu.VMEM)
    dma = pltpu.SemaphoreType.DMA
    scratch = [
        pltpu.VMEM((272, 128), F32),
        pltpu.VMEM((FLEN, 1024), BF16),
        pltpu.VMEM((256, K), F32),
        pltpu.VMEM((4, 512, 128), F32),
        pltpu.VMEM((16 * FR // GROUPS, 128), F32),
        pltpu.VMEM((256, FLEN), BF16),
        pltpu.VMEM((256, 512), F32),
        pltpu.VMEM((512, 256), F32),
        pltpu.VMEM((2, 32, 16, 256), BF16),
        pltpu.VMEM((16, 256), F32),
        pltpu.VMEM((2, 16, 16, 256), BF16),
        pltpu.VMEM((ITERS, 2, 256, 256), F32),
        pltpu.VMEM((ITERS, 2, 256, 256), F32),
        pltpu.VMEM((2, 32, 16, 256), BF16),
        pltpu.VMEM((63, 16, 256), BF16),
        pltpu.VMEM((ITERS, 2, 1, 256), F32),
        pltpu.VMEM((63, 1, 256), F32),
        pltpu.VMEM((1, 2, 1, K), F32),
        pltpu.VMEM((ITERS, 2, 1, K), F32),
        dma((4,)),
        dma((2,)),
        dma((GROUPS,)),
        dma((GROUPS,)),
        dma((3,)),
        dma((3,)),
        dma((3,)),
        dma((3,)),
        dma((ITERS, 2)),
        dma((ITERS, 2)),
        dma((8,)),
        dma((ITERS,)),
        dma((ITERS,)),
        dma((2,)),
        pltpu.SemaphoreType.REGULAR,
        pltpu.SemaphoreType.REGULAR,
    ]
    return pl.pallas_call(
        kernel,
        out_shape=(
            jax.ShapeDtypeStruct((256, K), F32),
            jax.ShapeDtypeStruct((512, 128), F32),
        ),
        in_specs=[hbm, pl.BlockSpec(memory_space=pltpu.SMEM), vmem, hbm, hbm, hbm],
        out_specs=(vmem, vmem),
        scratch_shapes=scratch,
        compiler_params=pltpu.CompilerParams(
            collective_id=0, has_side_effects=True, vmem_limit_bytes=48 * 2**20
        ),
    )(
        waveform.reshape(256, 128),
        starts,
        jnp.asarray(hann_window()),
        jnp.asarray(half_tables()),
        templates,
        activations,
    )


def solution(mesh):
    in_specs = (P(("tm", "freq")), P(("tm", "freq")), P("freq", None), P("tm", "freq"))
    out_specs = (P("freq", None), P("tm", "freq"))
    return jax.shard_map(shards, mesh=mesh, in_specs=in_specs, out_specs=out_specs, check_vma=False)
```

```python
import jax
import jax.numpy as jnp
import numpy as np
from jax import lax
from jax.experimental import pallas as pl
from jax.experimental.pallas import tpu as pltpu
from jax.sharding import PartitionSpec as P

FLEN = 2048
BINS = 1024
K = 512
ITERS = 2
SEG = 32768
FR = 128
GROUPS = 4
MESH = pl.DeviceIdType.MESH
F32 = jnp.float32
BF16 = jnp.bfloat16


def half_tables():
    row = np.arange(FLEN, dtype=np.int64)[:, None]
    tables = []
    for core in range(2):
        bins = np.concatenate([np.arange(256) + 256 * core, np.arange(256) + 512 + 256 * core])
        phase = ((row * bins[None, :]) % FLEN).astype(np.float32) * np.float32(2.0 * np.pi / FLEN)
        tables.append(np.concatenate([np.cos(phase), -np.sin(phase)], axis=1))
    return np.stack(tables).astype(jnp.bfloat16)


def hann_window():
    steps = np.arange(FLEN, dtype=np.float32) * np.float32(2.0 * np.pi / FLEN)
    return (np.float32(0.5) - np.float32(0.5) * np.cos(steps)).reshape(16, 128)


def hops(offset):
    return sum(min(v, 4 - v) for v in offset)


OFFSETS = sorted(
    [(dx, dy, dz) for dz in range(4) for dy in range(4) for dx in range(4) if dx or dy or dz],
    key=lambda offset: -hops(offset),
)


PLANE = sorted(
    [(dx, dy) for dy in range(4) for dx in range(4) if dx or dy],
    key=lambda offset: -hops(offset),
)


def dot(a, b, dims):
    return lax.dot_general(a, b, (dims, ((), ())), preferred_element_type=F32)


def kernel(
    wave_hbm, starts_hbm, window_hbm, table_hbm, templ_hbm, act_hbm, w_out, a_out,
    starts, window, wave, table, templ, acts, gathered, frames, energy, energy_t, wb, own_w, w_last,
    vb, part, part_got, t_send, t_got, tot, tot_z, z_got, xy_got, mass, mass_half,
    local_sem, rim_sem, frame_send, frame_recv, act_send, act_recv, w_send, w_recv,
    part_send, part_recv, t_sems, z_sems, xy_sems, mass_send, mass_recv, fin_sem, y_sem, z_sem,
):
    tm = lax.axis_index("tm")
    fr = lax.axis_index("freq")
    x, z, y_lo = lax.rem(tm, 4), lax.rem(lax.div(tm, 4), 4), lax.div(tm, 16)
    y_hi, core = lax.div(fr, 2), lax.rem(fr, 2)
    y = 2 * y_hi + y_lo
    xs = [lax.rem(x + d, 4) for d in range(4)]
    zs = [lax.rem(z + d, 4) for d in range(4)]
    ys = [lax.rem(y + d, 4) for d in range(4)]
    y_los = [lax.rem(v, 2) for v in ys]
    y_his = [lax.div(v, 2) for v in ys]

    def chip(dx, dy, dz):
        return (y_los[dy] * 16 + zs[dz] * 4 + xs[dx], y_his[dy] * 2 + core)

    def remote(src, dst, send, recv, device):
        return pltpu.make_async_remote_copy(
            src_ref=src, dst_ref=dst, send_sem=send, recv_sem=recv,
            device_id=device, device_id_type=MESH,
        )

    sibling = (tm, 2 * y_hi + 1 - core)
    across = (tm, 2 * (1 - y_hi) + core)
    beside = (lax.rem(tm + 16, 32), 2 * (1 - y_hi) + core)
    place = 4 * tm + fr
    following = lax.rem(place + 1, 128)
    previous = lax.rem(place + 127, 128)
    following = (lax.div(following, 4), lax.rem(following, 4))
    previous = (lax.div(previous, 4), lax.rem(previous, 4))

    copies = [
        pltpu.make_async_copy(wave_hbm, wave.at[pl.ds(0, 256)], local_sem.at[0]),
        pltpu.make_async_copy(act_hbm, acts.at[fr], local_sem.at[1]),
        pltpu.make_async_copy(templ_hbm, templ, local_sem.at[2]),
        pltpu.make_async_copy(table_hbm.at[core], table, local_sem.at[3]),
        pltpu.make_async_copy(starts_hbm, starts, local_sem.at[4]),
        pltpu.make_async_copy(window_hbm, window, local_sem.at[5]),
    ]
    barrier = pltpu.get_barrier_semaphore()
    axis_peers = [chip(d, 0, 0) for d in (1, 2, 3)]
    y_peers = [chip(0, d, 0) for d in (1, 2, 3)]
    z_peers = [chip(0, 0, d) for d in (1, 2, 3)]
    for device in [following, sibling] + axis_peers + y_peers + z_peers:
        pl.semaphore_signal(barrier, inc=1, device_id=device, device_id_type=MESH)
    for copy in copies:
        copy.start()
    copies[2].wait()
    for h in range(4):
        wb[h, pl.ds(16 * y_hi, 16)] = templ[:, 128 * h : 128 * h + 128].astype(BF16).reshape(16, 16, 128)
    mass[0, pl.ds(y_hi, 1)] = jnp.sum(templ[...], axis=0, keepdims=True).reshape(1, 1, K)
    g = 16 * y_hi + 4 * z + x
    for h in range(2):

        @pl.when(y_lo == h)
        def _():
            rows = pl.ds(pl.multiple_of(16 * (4 * z + x), 16), 16)
            for k in range(2):
                own_w[k] = templ[rows, 256 * k + 128 * h : 256 * k + 128 * h + 128]

    copies[0].wait()
    copies[1].wait()
    pl.semaphore_wait(barrier, 11)

    rim = remote(wave.at[pl.ds(0, 16)], wave.at[pl.ds(256, 16)], rim_sem.at[0], rim_sem.at[1], previous)
    rim.start()
    here = pl.ds(pl.multiple_of(256 * y_hi, 256), 256)
    there = pl.ds(pl.multiple_of(256 * (1 - y_hi), 256), 256)
    act_across = remote(acts.at[fr, there], acts.at[fr, there], act_send.at[0], act_recv.at[0], across)
    act_across.start()
    act_sibling = remote(acts.at[fr, here], acts.at[fr, here], act_send.at[1], act_recv.at[1], sibling)
    act_sibling.start()
    w_copies = []
    for h in range(4):
        rows = wb.at[h, pl.ds(16 * y_hi, 16)]
        w_copies.append(remote(rows, rows, w_send.at[h], w_recv.at[h], beside))
    w_copies.append(remote(mass.at[0, y_hi], mass.at[0, y_hi], w_send.at[4], w_recv.at[4], beside))
    for copy in w_copies:
        copy.start()
    for device in y_peers:
        pl.semaphore_signal(y_sem, inc=1, device_id=device, device_id_type=MESH)

    rim.wait()
    copies[4].wait()
    copies[5].wait()

    @pl.when(place == 127)
    def _():
        wave[pl.ds(256, 16)] = jnp.zeros((16, 128), F32)

    lanes = lax.broadcasted_iota(jnp.int32, (16, 128), 1)
    scale = window[...]
    size = FR // GROUPS
    frame_copies = []
    for group in range(GROUPS):

        def gather(i, carry):
            start = lax.rem(starts[group * size + i], SEG)
            row, shift = lax.div(start, 128), lax.rem(start, 128)
            low = wave[pl.ds(row, 16), :]
            high = wave[pl.ds(row + 1, 16), :]
            joined = jnp.where(lanes >= shift, low, high)
            rolled = pltpu.roll(joined, lax.rem(128 - shift, 128), 1)
            gathered[pl.ds(i, 16, stride=size), :] = rolled * scale
            return carry

        lax.fori_loop(0, size, gather, 0, unroll=8)
        rows = pl.ds(pl.multiple_of(FR * core + group * size, size), size)
        for i in range(16):
            frames[rows, 128 * i : 128 * i + 128] = gathered[size * i : size * i + size, :].astype(BF16)
        copy = remote(frames.at[rows], frames.at[rows], frame_send.at[group], frame_recv.at[group], sibling)
        copy.start()
        frame_copies.append(copy)

    act_across.wait()
    far = 2 * (1 - y_hi) + core
    act_pass = remote(acts.at[far, here], acts.at[far, here], act_send.at[2], act_recv.at[2], sibling)
    act_pass.start()
    pl.semaphore_wait(y_sem, 3)
    for device in z_peers:
        pl.semaphore_signal(z_sem, inc=1, device_id=device, device_id_type=MESH)
    copies[3].wait()
    for copy in frame_copies:
        copy.wait()
    for j in range(2):
        cos = dot(frames[...], table[:, 256 * j : 256 * j + 256], ((1,), (0,)))
        sin = dot(frames[...], table[:, 512 + 256 * j : 768 + 256 * j], ((1,), (0,)))
        square = (cos * cos + sin * sin) * 0.25
        energy[:, 256 * j : 256 * j + 256] = square
        energy_t[256 * j : 256 * j + 256, :] = square.T
    for copy in w_copies:
        copy.wait()
    act_sibling.wait()
    act_pass.wait()
    pl.semaphore_wait(z_sem, 3)

    for t in range(ITERS):
        w_half = [
            jnp.concatenate([wb[2 * h].reshape(512, 128), wb[2 * h + 1].reshape(512, 128)], axis=1)
            for h in range(2)
        ]
        if t == 0:
            half = mass[0, 0] + mass[0, 1]
        else:
            half = jnp.concatenate(halves, axis=1)
        mass_half[t, 0] = half
        mass_copy = remote(mass_half.at[t, 0], mass_half.at[t, 1], mass_send.at[t], mass_recv.at[t], sibling)
        mass_copy.start()
        hb = [acts[f, here].astype(BF16) for f in range(4)]
        hb = [jnp.concatenate(hb[:2], axis=1), jnp.concatenate(hb[2:], axis=1)]
        rebuilt = dot(hb[0], w_half[0], ((1,), (1,))) + dot(hb[1], w_half[1], ((1,), (1,)))
        ratios = (energy[...] / rebuilt).astype(BF16)
        part_copies = []
        for h in range(2):
            part[t, h] = dot(ratios, w_half[h], ((1,), (0,)))
            copy = remote(part.at[t, h], part_got.at[t, h], part_send.at[t, h], part_recv.at[t, h], sibling)
            copy.start()
            part_copies.append(copy)
        mass_copy.wait()
        inverse = 1.0 / (mass_half[t, 0] + mass_half[t, 1])
        hb = []
        for h in range(2):
            part_copies[h].wait()
            factor = (part[t, h] + part_got[t, h]) * inverse[:, 256 * h : 256 * h + 256]
            pieces = []
            for k in range(2):
                new = acts[2 * h + k, here] * factor[:, 128 * k : 128 * k + 128]
                acts[2 * h + k, here] = new
                pieces.append(new.astype(BF16))
            hb.append(jnp.concatenate(pieces, axis=1))
            tot[t, :, 256 * h : 256 * h + 256] = jnp.sum(hb[h].astype(F32), axis=0, keepdims=True)
        if t == ITERS - 1:
            final = remote(acts.at[far, here], acts.at[far, here], fin_sem.at[0], fin_sem.at[1], across)
            final.start()

        for slot in range(3):
            remote(tot.at[t], z_got.at[t, slot], z_sems.at[0, t], z_sems.at[1, t], z_peers[slot]).start()

        rebuilt = dot(w_half[0], hb[0], ((1,), (1,))) + dot(w_half[1], hb[1], ((1,), (1,)))
        ratios = (energy_t[...] / rebuilt).astype(BF16)
        for h in range(2):
            term = dot(ratios, hb[h], ((1,), (0,))).astype(BF16)
            for k in range(2):
                t_send[2 * h + k] = term[:, 128 * k : 128 * k + 128].reshape(32, 16, 128)
            for slot, (dx, dy, dz) in enumerate(OFFSETS):
                owner = 16 * y_his[dy] + 4 * zs[dz] + xs[dx]
                remote(
                    t_send.at[2 * h + y_los[dy], owner], t_got.at[h, slot],
                    t_sems.at[0, h], t_sems.at[1, h], chip(dx, dy, dz),
                ).start()
        for s in range(2):
            pltpu.make_async_copy(z_got.at[t], z_got.at[t], z_sems.at[s, t]).wait()
        plane = tot[t]
        for slot in range(3):
            plane = plane + z_got[t, slot]
        tot_z[t] = plane
        for slot, (dx, dy) in enumerate(PLANE):
            remote(
                tot_z.at[t], xy_got.at[t, slot], xy_sems.at[0, t], xy_sems.at[1, t], chip(dx, dy, 0)
            ).start()

        for h in range(2):
            summed = t_send[2 * h + y_lo, g].astype(F32)
            for s in range(2):
                pltpu.make_async_copy(t_got.at[h], t_got.at[h], t_sems.at[s, h]).wait()
            summed = summed + jnp.sum(t_got[h].astype(F32), axis=0)
            own_w[h] = own_w[h] * summed
            if t < ITERS - 1:
                mine = vb.at[2 * h + y_lo, g]
                peers = [chip(*offset) for offset in OFFSETS]
            else:
                mine = w_last.at[2 * h + y_lo, 4 * z + x]
                peers = [
                    (16 * (1 - y_lo if dy else y_lo) + 4 * zs[dz] + xs[dx], fr)
                    for dx, dy, dz in OFFSETS
                    if dy < 2
                ]
            mine[...] = own_w[h].astype(BF16)
            for device in peers:
                remote(mine, mine, t_sems.at[2, h], t_sems.at[3, h], device).start()
        if t == ITERS - 1:
            final.wait()
            a_copy = pltpu.make_async_copy(acts.at[fr], a_out, local_sem.at[1])
            a_copy.start()
        for s in range(2):
            pltpu.make_async_copy(xy_got.at[t], xy_got.at[t], xy_sems.at[s, t]).wait()
        inv_total = 1.0 / (tot_z[t] + jnp.sum(xy_got[t], axis=0))
        if t < ITERS - 1:
            for h in range(2):
                low = inv_total[:, 256 * h : 256 * h + 128]
                high = inv_total[:, 256 * h + 128 : 256 * h + 256]
                own_w[h] = own_w[h] * jnp.where(y_lo == 0, low, high)
        halves = []
        for h in range(2):
            arrived = t_got.at[h] if t < ITERS - 1 else t_got.at[h, pl.ds(0, 31)]
            for s in range(2, 4):
                pltpu.make_async_copy(arrived, arrived, t_sems.at[s, h]).wait()
            for q in (2 * h, 2 * h + 1):
                scale_q = inv_total[:, 128 * q : 128 * q + 128]
                if t < ITERS - 1:
                    block = vb[q].reshape(512, 128).astype(F32) * scale_q
                    halves.append(jnp.sum(block, axis=0, keepdims=True))
                    wb[q] = block.astype(BF16).reshape(32, 16, 128)
                else:
                    block = w_last[q].reshape(256, 128).astype(F32)
                    w_out[:, 128 * q : 128 * q + 128] = block * scale_q
        if t == ITERS - 1:
            a_copy.wait()


def shards(waveform, starts, templates, activations):
    hbm = pl.BlockSpec(memory_space=pltpu.HBM)
    vmem = pl.BlockSpec(memory_space=pltpu.VMEM)
    dma = pltpu.SemaphoreType.DMA
    scratch = [
        pltpu.SMEM((FR,), jnp.int32),
        pltpu.VMEM((16, 128), F32),
        pltpu.VMEM((272, 128), F32),
        pltpu.VMEM((FLEN, 1024), BF16),
        pltpu.VMEM((256, K), F32),
        pltpu.VMEM((4, 512, 128), F32),
        pltpu.VMEM((16 * FR // GROUPS, 128), F32),
        pltpu.VMEM((256, FLEN), BF16),
        pltpu.VMEM((256, 512), F32),
        pltpu.VMEM((512, 256), F32),
        pltpu.VMEM((4, 32, 16, 128), BF16),
        pltpu.VMEM((2, 16, 128), F32),
        pltpu.VMEM((4, 16, 16, 128), BF16),
        pltpu.VMEM((4, 32, 16, 128), BF16),
        pltpu.VMEM((ITERS, 2, 256, 256), F32),
        pltpu.VMEM((ITERS, 2, 256, 256), F32),
        pltpu.VMEM((4, 32, 16, 128), BF16),
        pltpu.VMEM((2, 63, 16, 128), BF16),
        pltpu.VMEM((ITERS, 1, K), F32),
        pltpu.VMEM((ITERS, 1, K), F32),
        pltpu.VMEM((ITERS, 3, 1, K), F32),
        pltpu.VMEM((ITERS, 15, 1, K), F32),
        pltpu.VMEM((1, 2, 1, K), F32),
        pltpu.VMEM((ITERS, 2, 1, K), F32),
        dma((6,)),
        dma((2,)),
        dma((GROUPS,)),
        dma((GROUPS,)),
        dma((3,)),
        dma((3,)),
        dma((5,)),
        dma((5,)),
        dma((ITERS, 2)),
        dma((ITERS, 2)),
        dma((4, 2)),
        dma((2, ITERS)),
        dma((2, ITERS)),
        dma((ITERS,)),
        dma((ITERS,)),
        dma((2,)),
        pltpu.SemaphoreType.REGULAR,
        pltpu.SemaphoreType.REGULAR,
    ]
    return pl.pallas_call(
        kernel,
        out_shape=(
            jax.ShapeDtypeStruct((256, K), F32),
            jax.ShapeDtypeStruct((512, 128), F32),
        ),
        in_specs=[hbm] * 6,
        out_specs=(vmem, hbm),
        scratch_shapes=scratch,
        compiler_params=pltpu.CompilerParams(
            collective_id=0, has_side_effects=True, vmem_limit_bytes=60 * 2**20
        ),
    )(
        waveform.reshape(256, 128),
        starts,
        jnp.asarray(hann_window()),
        jnp.asarray(half_tables()),
        templates,
        activations,
    )


def solution(mesh):
    in_specs = (P(("tm", "freq")), P(("tm", "freq")), P("freq", None), P("tm", "freq"))
    out_specs = (P("freq", None), P("tm", "freq"))
    return jax.shard_map(shards, mesh=mesh, in_specs=in_specs, out_specs=out_specs, check_vma=False)
```

```python
import jax
import jax.numpy as jnp
import numpy as np
from jax import lax
from jax.experimental import pallas as pl
from jax.experimental.pallas import tpu as pltpu
from jax.sharding import PartitionSpec as P

FLEN = 2048
BINS = 1024
K = 512
ITERS = 2
SEG = 32768
FR = 128
GROUPS = 4
MESH = pl.DeviceIdType.MESH
F32 = jnp.float32
BF16 = jnp.bfloat16


def half_tables():
    row = np.arange(FLEN, dtype=np.int64)[:, None]
    tables = []
    for core in range(2):
        bins = np.concatenate([np.arange(256) + 256 * core, np.arange(256) + 512 + 256 * core])
        phase = ((row * bins[None, :]) % FLEN).astype(np.float32) * np.float32(2.0 * np.pi / FLEN)
        tables.append(np.concatenate([np.cos(phase), -np.sin(phase)], axis=1))
    return np.stack(tables).astype(jnp.bfloat16)


def hann_window():
    steps = np.arange(FLEN, dtype=np.float32) * np.float32(2.0 * np.pi / FLEN)
    return (np.float32(0.5) - np.float32(0.5) * np.cos(steps)).reshape(16, 128)


def hops(offset):
    return sum(min(v, 4 - v) for v in offset)


OFFSETS = sorted(
    [(dx, dy, dz) for dz in range(4) for dy in range(4) for dx in range(4) if dx or dy or dz],
    key=lambda offset: -hops(offset),
)


PLANE = sorted(
    [(dx, dy) for dy in range(4) for dx in range(4) if dx or dy],
    key=lambda offset: -hops(offset),
)


def dot(a, b, dims):
    return lax.dot_general(a, b, (dims, ((), ())), preferred_element_type=F32)


def kernel(
    wave_hbm, starts_hbm, window_hbm, table_hbm, templ_hbm, act_hbm, w_out, a_out,
    starts, window, wave, table, templ, acts, gathered, frames, energy, energy_t, wb, own_w, w_last,
    vb, part, part_got, t_send, t_got, tot, tot_z, z_got, xy_got, mass, mass_half,
    local_sem, rim_sem, frame_send, frame_recv, act_send, act_recv, w_send, w_recv,
    part_send, part_recv, t_sems, z_sems, xy_sems, mass_send, mass_recv, fin_sem, y_sem, z_sem,
):
    tm = lax.axis_index("tm")
    fr = lax.axis_index("freq")
    x, z, y_lo = lax.rem(tm, 4), lax.rem(lax.div(tm, 4), 4), lax.div(tm, 16)
    y_hi, core = lax.div(fr, 2), lax.rem(fr, 2)
    y = 2 * y_hi + y_lo
    xs = [lax.rem(x + d, 4) for d in range(4)]
    zs = [lax.rem(z + d, 4) for d in range(4)]
    ys = [lax.rem(y + d, 4) for d in range(4)]
    y_los = [lax.rem(v, 2) for v in ys]
    y_his = [lax.div(v, 2) for v in ys]

    def chip(dx, dy, dz):
        return (y_los[dy] * 16 + zs[dz] * 4 + xs[dx], y_his[dy] * 2 + core)

    def remote(src, dst, send, recv, device):
        return pltpu.make_async_remote_copy(
            src_ref=src, dst_ref=dst, send_sem=send, recv_sem=recv,
            device_id=device, device_id_type=MESH,
        )

    sibling = (tm, 2 * y_hi + 1 - core)
    across = (tm, 2 * (1 - y_hi) + core)
    beside = (lax.rem(tm + 16, 32), 2 * (1 - y_hi) + core)
    place = 4 * tm + fr
    following = lax.rem(place + 1, 128)
    previous = lax.rem(place + 127, 128)
    following = (lax.div(following, 4), lax.rem(following, 4))
    previous = (lax.div(previous, 4), lax.rem(previous, 4))

    copies = [
        pltpu.make_async_copy(wave_hbm, wave.at[pl.ds(0, 256)], local_sem.at[0]),
        pltpu.make_async_copy(act_hbm, acts.at[fr], local_sem.at[1]),
        pltpu.make_async_copy(templ_hbm, templ, local_sem.at[2]),
        pltpu.make_async_copy(table_hbm.at[core], table, local_sem.at[3]),
        pltpu.make_async_copy(starts_hbm, starts, local_sem.at[4]),
        pltpu.make_async_copy(window_hbm, window, local_sem.at[5]),
    ]
    barrier = pltpu.get_barrier_semaphore()
    axis_peers = [chip(d, 0, 0) for d in (1, 2, 3)]
    y_peers = [chip(0, d, 0) for d in (1, 2, 3)]
    z_peers = [chip(0, 0, d) for d in (1, 2, 3)]
    for device in [following, sibling] + axis_peers + y_peers + z_peers:
        pl.semaphore_signal(barrier, inc=1, device_id=device, device_id_type=MESH)
    for copy in copies:
        copy.start()
    copies[2].wait()
    for h in range(4):
        wb[h, pl.ds(16 * y_hi, 16)] = templ[:, 128 * h : 128 * h + 128].astype(BF16).reshape(16, 16, 128)
    mass[0, pl.ds(y_hi, 1)] = jnp.sum(templ[...], axis=0, keepdims=True).reshape(1, 1, K)
    g = 16 * y_hi + 4 * z + x
    for h in range(2):

        @pl.when(y_lo == h)
        def _():
            rows = pl.ds(pl.multiple_of(16 * (4 * z + x), 16), 16)
            for k in range(2):
                own_w[k] = templ[rows, 256 * k + 128 * h : 256 * k + 128 * h + 128]

    copies[0].wait()
    copies[1].wait()
    pl.semaphore_wait(barrier, 11)

    rim = remote(wave.at[pl.ds(0, 16)], wave.at[pl.ds(256, 16)], rim_sem.at[0], rim_sem.at[1], previous)
    rim.start()
    here = pl.ds(pl.multiple_of(256 * y_hi, 256), 256)
    there = pl.ds(pl.multiple_of(256 * (1 - y_hi), 256), 256)
    act_across = remote(acts.at[fr, there], acts.at[fr, there], act_send.at[0], act_recv.at[0], across)
    act_across.start()
    act_sibling = remote(acts.at[fr, here], acts.at[fr, here], act_send.at[1], act_recv.at[1], sibling)
    act_sibling.start()
    w_copies = []
    for h in range(4):
        rows = wb.at[h, pl.ds(16 * y_hi, 16)]
        w_copies.append(remote(rows, rows, w_send.at[h], w_recv.at[h], beside))
    w_copies.append(remote(mass.at[0, y_hi], mass.at[0, y_hi], w_send.at[4], w_recv.at[4], beside))
    for copy in w_copies:
        copy.start()
    for device in y_peers:
        pl.semaphore_signal(y_sem, inc=1, device_id=device, device_id_type=MESH)

    rim.wait()
    copies[4].wait()
    copies[5].wait()

    @pl.when(place == 127)
    def _():
        wave[pl.ds(256, 16)] = jnp.zeros((16, 128), F32)

    lanes = lax.broadcasted_iota(jnp.int32, (16, 128), 1)
    scale = window[...]
    size = FR // GROUPS
    frame_copies = []
    for group in range(GROUPS):

        def gather(i, carry):
            start = lax.rem(starts[group * size + i], SEG)
            row, shift = lax.div(start, 128), lax.rem(start, 128)
            low = wave[pl.ds(row, 16), :]
            high = wave[pl.ds(row + 1, 16), :]
            joined = jnp.where(lanes >= shift, low, high)
            rolled = pltpu.roll(joined, lax.rem(128 - shift, 128), 1)
            gathered[pl.ds(i, 16, stride=size), :] = rolled * scale
            return carry

        lax.fori_loop(0, size, gather, 0, unroll=8)
        rows = pl.ds(pl.multiple_of(FR * core + group * size, size), size)
        for i in range(16):
            frames[rows, 128 * i : 128 * i + 128] = gathered[size * i : size * i + size, :].astype(BF16)
        copy = remote(frames.at[rows], frames.at[rows], frame_send.at[group], frame_recv.at[group], sibling)
        copy.start()
        frame_copies.append(copy)

    act_across.wait()
    far = 2 * (1 - y_hi) + core
    act_pass = remote(acts.at[far, here], acts.at[far, here], act_send.at[2], act_recv.at[2], sibling)
    act_pass.start()
    pl.semaphore_wait(y_sem, 3)
    for device in z_peers:
        pl.semaphore_signal(z_sem, inc=1, device_id=device, device_id_type=MESH)
    copies[3].wait()
    for copy in frame_copies:
        copy.wait()
    for j in range(2):
        cos = dot(frames[...], table[:, 256 * j : 256 * j + 256], ((1,), (0,)))
        sin = dot(frames[...], table[:, 512 + 256 * j : 768 + 256 * j], ((1,), (0,)))
        square = (cos * cos + sin * sin) * 0.25
        energy[:, 256 * j : 256 * j + 256] = square
        energy_t[256 * j : 256 * j + 256, :] = square.T
    for copy in w_copies:
        copy.wait()
    act_sibling.wait()
    act_pass.wait()
    pl.semaphore_wait(z_sem, 3)

    for t in range(ITERS):
        w_half = [
            jnp.concatenate([wb[2 * h].reshape(512, 128), wb[2 * h + 1].reshape(512, 128)], axis=1)
            for h in range(2)
        ]
        if t == 0:
            half = mass[0, 0] + mass[0, 1]
        else:
            half = jnp.concatenate(halves, axis=1)
        mass_half[t, 0] = half
        mass_copy = remote(mass_half.at[t, 0], mass_half.at[t, 1], mass_send.at[t], mass_recv.at[t], sibling)
        mass_copy.start()
        hb = [acts[f, here].astype(BF16) for f in range(4)]
        hb = [jnp.concatenate(hb[:2], axis=1), jnp.concatenate(hb[2:], axis=1)]
        rebuilt = dot(hb[0], w_half[0], ((1,), (1,))) + dot(hb[1], w_half[1], ((1,), (1,)))
        ratios = (energy[...] / rebuilt).astype(BF16)
        part_copies = []
        for h in range(2):
            part[t, h] = dot(ratios, w_half[h], ((1,), (0,)))
            copy = remote(part.at[t, h], part_got.at[t, h], part_send.at[t, h], part_recv.at[t, h], sibling)
            copy.start()
            part_copies.append(copy)
        mass_copy.wait()
        inverse = 1.0 / (mass_half[t, 0] + mass_half[t, 1])
        hb = []
        for h in range(2):
            part_copies[h].wait()
            factor = (part[t, h] + part_got[t, h]) * inverse[:, 256 * h : 256 * h + 256]
            pieces = []
            for k in range(2):
                new = acts[2 * h + k, here] * factor[:, 128 * k : 128 * k + 128]
                acts[2 * h + k, here] = new
                pieces.append(new.astype(BF16))
            hb.append(jnp.concatenate(pieces, axis=1))
            tot[t, :, 256 * h : 256 * h + 256] = jnp.sum(hb[h].astype(F32), axis=0, keepdims=True)

        for slot in range(3):
            remote(tot.at[t], z_got.at[t, slot], z_sems.at[0, t], z_sems.at[1, t], z_peers[slot]).start()

        rebuilt = dot(w_half[0], hb[0], ((1,), (1,))) + dot(w_half[1], hb[1], ((1,), (1,)))
        ratios = (energy_t[...] / rebuilt).astype(BF16)
        for h in range(2):
            term = dot(ratios, hb[h], ((1,), (0,))).astype(BF16)
            for k in range(2):
                t_send[2 * h + k] = term[:, 128 * k : 128 * k + 128].reshape(32, 16, 128)
            for slot, (dx, dy, dz) in enumerate(OFFSETS):
                owner = 16 * y_his[dy] + 4 * zs[dz] + xs[dx]
                remote(
                    t_send.at[2 * h + y_los[dy], owner], t_got.at[h, slot],
                    t_sems.at[0, h], t_sems.at[1, h], chip(dx, dy, dz),
                ).start()
        for s in range(2):
            pltpu.make_async_copy(z_got.at[t], z_got.at[t], z_sems.at[s, t]).wait()
        plane = tot[t]
        for slot in range(3):
            plane = plane + z_got[t, slot]
        tot_z[t] = plane
        for slot, (dx, dy) in enumerate(PLANE):
            remote(
                tot_z.at[t], xy_got.at[t, slot], xy_sems.at[0, t], xy_sems.at[1, t], chip(dx, dy, 0)
            ).start()

        if t == ITERS - 1:
            final = remote(acts.at[far, here], acts.at[far, here], fin_sem.at[0], fin_sem.at[1], across)
            final.start()

        for h in range(2):
            summed = t_send[2 * h + y_lo, g].astype(F32)
            for s in range(2):
                pltpu.make_async_copy(t_got.at[h], t_got.at[h], t_sems.at[s, h]).wait()
            summed = summed + jnp.sum(t_got[h].astype(F32), axis=0)
            own_w[h] = own_w[h] * summed
            if t < ITERS - 1:
                mine = vb.at[2 * h + y_lo, g]
                peers = [chip(*offset) for offset in OFFSETS]
            else:
                mine = w_last.at[2 * h + y_lo, 4 * z + x]
                peers = [
                    (16 * (1 - y_lo if dy else y_lo) + 4 * zs[dz] + xs[dx], fr)
                    for dx, dy, dz in OFFSETS
                    if dy < 2
                ]
            mine[...] = own_w[h].astype(BF16)
            for device in peers:
                remote(mine, mine, t_sems.at[2, h], t_sems.at[3, h], device).start()
        if t == ITERS - 1:
            final.wait()
            a_copy = pltpu.make_async_copy(acts.at[fr], a_out, local_sem.at[1])
            a_copy.start()
        for s in range(2):
            pltpu.make_async_copy(xy_got.at[t], xy_got.at[t], xy_sems.at[s, t]).wait()
        inv_total = 1.0 / (tot_z[t] + jnp.sum(xy_got[t], axis=0))
        if t < ITERS - 1:
            for h in range(2):
                low = inv_total[:, 256 * h : 256 * h + 128]
                high = inv_total[:, 256 * h + 128 : 256 * h + 256]
                own_w[h] = own_w[h] * jnp.where(y_lo == 0, low, high)
        halves = []
        for h in range(2):
            arrived = t_got.at[h] if t < ITERS - 1 else t_got.at[h, pl.ds(0, 31)]
            for s in range(2, 4):
                pltpu.make_async_copy(arrived, arrived, t_sems.at[s, h]).wait()
            for q in (2 * h, 2 * h + 1):
                scale_q = inv_total[:, 128 * q : 128 * q + 128]
                if t < ITERS - 1:
                    block = vb[q].reshape(512, 128).astype(F32) * scale_q
                    halves.append(jnp.sum(block, axis=0, keepdims=True))
                    wb[q] = block.astype(BF16).reshape(32, 16, 128)
                else:
                    block = w_last[q].reshape(256, 128).astype(F32)
                    w_out[:, 128 * q : 128 * q + 128] = block * scale_q
        if t == ITERS - 1:
            a_copy.wait()


def shards(waveform, starts, templates, activations):
    hbm = pl.BlockSpec(memory_space=pltpu.HBM)
    vmem = pl.BlockSpec(memory_space=pltpu.VMEM)
    dma = pltpu.SemaphoreType.DMA
    scratch = [
        pltpu.SMEM((FR,), jnp.int32),
        pltpu.VMEM((16, 128), F32),
        pltpu.VMEM((272, 128), F32),
        pltpu.VMEM((FLEN, 1024), BF16),
        pltpu.VMEM((256, K), F32),
        pltpu.VMEM((4, 512, 128), F32),
        pltpu.VMEM((16 * FR // GROUPS, 128), F32),
        pltpu.VMEM((256, FLEN), BF16),
        pltpu.VMEM((256, 512), F32),
        pltpu.VMEM((512, 256), F32),
        pltpu.VMEM((4, 32, 16, 128), BF16),
        pltpu.VMEM((2, 16, 128), F32),
        pltpu.VMEM((4, 16, 16, 128), BF16),
        pltpu.VMEM((4, 32, 16, 128), BF16),
        pltpu.VMEM((ITERS, 2, 256, 256), F32),
        pltpu.VMEM((ITERS, 2, 256, 256), F32),
        pltpu.VMEM((4, 32, 16, 128), BF16),
        pltpu.VMEM((2, 63, 16, 128), BF16),
        pltpu.VMEM((ITERS, 1, K), F32),
        pltpu.VMEM((ITERS, 1, K), F32),
        pltpu.VMEM((ITERS, 3, 1, K), F32),
        pltpu.VMEM((ITERS, 15, 1, K), F32),
        pltpu.VMEM((1, 2, 1, K), F32),
        pltpu.VMEM((ITERS, 2, 1, K), F32),
        dma((6,)),
        dma((2,)),
        dma((GROUPS,)),
        dma((GROUPS,)),
        dma((3,)),
        dma((3,)),
        dma((5,)),
        dma((5,)),
        dma((ITERS, 2)),
        dma((ITERS, 2)),
        dma((4, 2)),
        dma((2, ITERS)),
        dma((2, ITERS)),
        dma((ITERS,)),
        dma((ITERS,)),
        dma((2,)),
        pltpu.SemaphoreType.REGULAR,
        pltpu.SemaphoreType.REGULAR,
    ]
    return pl.pallas_call(
        kernel,
        out_shape=(
            jax.ShapeDtypeStruct((256, K), F32),
            jax.ShapeDtypeStruct((512, 128), F32),
        ),
        in_specs=[hbm] * 6,
        out_specs=(vmem, hbm),
        scratch_shapes=scratch,
        compiler_params=pltpu.CompilerParams(
            collective_id=0, has_side_effects=True, vmem_limit_bytes=60 * 2**20
        ),
    )(
        waveform.reshape(256, 128),
        starts,
        jnp.asarray(hann_window()),
        jnp.asarray(half_tables()),
        templates,
        activations,
    )


def solution(mesh):
    in_specs = (P(("tm", "freq")), P(("tm", "freq")), P("freq", None), P("tm", "freq"))
    out_specs = (P("freq", None), P("tm", "freq"))
    return jax.shard_map(shards, mesh=mesh, in_specs=in_specs, out_specs=out_specs, check_vma=False)
```

```python
import jax
import jax.numpy as jnp
import numpy as np
from jax import lax
from jax.experimental import pallas as pl
from jax.experimental.pallas import tpu as pltpu
from jax.sharding import PartitionSpec as P

FLEN = 2048
BINS = 1024
K = 512
ITERS = 2
SEG = 32768
FR = 128
GROUPS = 4
MESH = pl.DeviceIdType.MESH
F32 = jnp.float32
BF16 = jnp.bfloat16


def half_tables():
    row = np.arange(FLEN, dtype=np.int64)[:, None]
    tables = []
    for core in range(2):
        bins = np.concatenate([np.arange(256) + 256 * core, np.arange(256) + 512 + 256 * core])
        phase = ((row * bins[None, :]) % FLEN).astype(np.float32) * np.float32(2.0 * np.pi / FLEN)
        tables.append(np.concatenate([np.cos(phase), -np.sin(phase)], axis=1))
    return np.stack(tables).astype(jnp.bfloat16)


def hann_window():
    steps = np.arange(FLEN, dtype=np.float32) * np.float32(2.0 * np.pi / FLEN)
    return (np.float32(0.5) - np.float32(0.5) * np.cos(steps)).reshape(16, 128)


def hops(offset):
    return sum(min(v, 4 - v) for v in offset)


OFFSETS = sorted(
    [(dx, dy, dz) for dz in range(4) for dy in range(4) for dx in range(4) if dx or dy or dz],
    key=lambda offset: -hops(offset),
)


PLANE = sorted(
    [(dx, dy) for dy in range(4) for dx in range(4) if dx or dy],
    key=lambda offset: -hops(offset),
)


def dot(a, b, dims):
    return lax.dot_general(a, b, (dims, ((), ())), preferred_element_type=F32)


def kernel(
    wave_hbm, starts_hbm, window_hbm, table_hbm, templ_hbm, act_hbm, w_out, a_out,
    starts, window, wave, table, templ, acts, gathered, frames, energy, energy_t, wb, own_w, w_last,
    vb, part, part_got, t_send, t_got, tot, tot_z, z_got, xy_got, mass, mass_half,
    local_sem, rim_sem, frame_send, frame_recv, act_send, act_recv, w_send, w_recv,
    part_send, part_recv, t_sems, z_sems, xy_sems, mass_send, mass_recv, fin_sem, y_sem, z_sem,
):
    tm = lax.axis_index("tm")
    fr = lax.axis_index("freq")
    x, z, y_lo = lax.rem(tm, 4), lax.rem(lax.div(tm, 4), 4), lax.div(tm, 16)
    y_hi, core = lax.div(fr, 2), lax.rem(fr, 2)
    y = 2 * y_hi + y_lo
    xs = [lax.rem(x + d, 4) for d in range(4)]
    zs = [lax.rem(z + d, 4) for d in range(4)]
    ys = [lax.rem(y + d, 4) for d in range(4)]
    y_los = [lax.rem(v, 2) for v in ys]
    y_his = [lax.div(v, 2) for v in ys]

    def chip(dx, dy, dz):
        return (y_los[dy] * 16 + zs[dz] * 4 + xs[dx], y_his[dy] * 2 + core)

    def remote(src, dst, send, recv, device):
        return pltpu.make_async_remote_copy(
            src_ref=src, dst_ref=dst, send_sem=send, recv_sem=recv,
            device_id=device, device_id_type=MESH,
        )

    sibling = (tm, 2 * y_hi + 1 - core)
    across = (tm, 2 * (1 - y_hi) + core)
    beside = (lax.rem(tm + 16, 32), 2 * (1 - y_hi) + core)
    place = 4 * tm + fr
    following = lax.rem(place + 1, 128)
    previous = lax.rem(place + 127, 128)
    following = (lax.div(following, 4), lax.rem(following, 4))
    previous = (lax.div(previous, 4), lax.rem(previous, 4))

    copies = [
        pltpu.make_async_copy(wave_hbm, wave.at[pl.ds(0, 256)], local_sem.at[0]),
        pltpu.make_async_copy(act_hbm, acts.at[fr], local_sem.at[1]),
        pltpu.make_async_copy(templ_hbm, templ, local_sem.at[2]),
        pltpu.make_async_copy(table_hbm.at[core], table, local_sem.at[3]),
        pltpu.make_async_copy(starts_hbm, starts, local_sem.at[4]),
        pltpu.make_async_copy(window_hbm, window, local_sem.at[5]),
    ]
    barrier = pltpu.get_barrier_semaphore()
    axis_peers = [chip(d, 0, 0) for d in (1, 2, 3)]
    y_peers = [chip(0, d, 0) for d in (1, 2, 3)]
    z_peers = [chip(0, 0, d) for d in (1, 2, 3)]
    for device in [following, sibling] + axis_peers + y_peers + z_peers:
        pl.semaphore_signal(barrier, inc=1, device_id=device, device_id_type=MESH)
    for copy in copies:
        copy.start()
    copies[2].wait()
    for h in range(4):
        wb[h, pl.ds(16 * y_hi, 16)] = templ[:, 128 * h : 128 * h + 128].astype(BF16).reshape(16, 16, 128)
    mass[0, pl.ds(y_hi, 1)] = jnp.sum(templ[...], axis=0, keepdims=True).reshape(1, 1, K)
    g = 16 * y_hi + 4 * z + x
    for h in range(2):

        @pl.when(y_lo == h)
        def _():
            rows = pl.ds(pl.multiple_of(16 * (4 * z + x), 16), 16)
            for k in range(2):
                own_w[k] = templ[rows, 256 * k + 128 * h : 256 * k + 128 * h + 128]

    copies[0].wait()
    copies[1].wait()
    pl.semaphore_wait(barrier, 11)

    rim = remote(wave.at[pl.ds(0, 16)], wave.at[pl.ds(256, 16)], rim_sem.at[0], rim_sem.at[1], previous)
    rim.start()
    here = pl.ds(pl.multiple_of(256 * y_hi, 256), 256)
    there = pl.ds(pl.multiple_of(256 * (1 - y_hi), 256), 256)
    act_across = remote(acts.at[fr, there], acts.at[fr, there], act_send.at[0], act_recv.at[0], across)
    act_across.start()
    act_sibling = remote(acts.at[fr, here], acts.at[fr, here], act_send.at[1], act_recv.at[1], sibling)
    act_sibling.start()
    w_copies = []
    for h in range(4):
        rows = wb.at[h, pl.ds(16 * y_hi, 16)]
        w_copies.append(remote(rows, rows, w_send.at[h], w_recv.at[h], beside))
    w_copies.append(remote(mass.at[0, y_hi], mass.at[0, y_hi], w_send.at[4], w_recv.at[4], beside))
    for copy in w_copies:
        copy.start()
    for device in y_peers:
        pl.semaphore_signal(y_sem, inc=1, device_id=device, device_id_type=MESH)

    rim.wait()
    copies[4].wait()
    copies[5].wait()

    @pl.when(place == 127)
    def _():
        wave[pl.ds(256, 16)] = jnp.zeros((16, 128), F32)

    lanes = lax.broadcasted_iota(jnp.int32, (16, 128), 1)
    scale = window[...]
    size = FR // GROUPS
    frame_copies = []
    for group in range(GROUPS):

        def gather(i, carry):
            start = lax.rem(starts[group * size + i], SEG)
            row, shift = lax.div(start, 128), lax.rem(start, 128)
            low = wave[pl.ds(row, 16), :]
            high = wave[pl.ds(row + 1, 16), :]
            joined = jnp.where(lanes >= shift, low, high)
            rolled = pltpu.roll(joined, lax.rem(128 - shift, 128), 1)
            gathered[pl.ds(i, 16, stride=size), :] = rolled * scale
            return carry

        lax.fori_loop(0, size, gather, 0, unroll=8)
        rows = pl.ds(pl.multiple_of(FR * core + group * size, size), size)
        for i in range(16):
            frames[rows, 128 * i : 128 * i + 128] = gathered[size * i : size * i + size, :].astype(BF16)
        copy = remote(frames.at[rows], frames.at[rows], frame_send.at[group], frame_recv.at[group], sibling)
        copy.start()
        frame_copies.append(copy)

    act_across.wait()
    far = 2 * (1 - y_hi) + core
    act_pass = remote(acts.at[far, here], acts.at[far, here], act_send.at[2], act_recv.at[2], sibling)
    act_pass.start()
    pl.semaphore_wait(y_sem, 3)
    for device in z_peers:
        pl.semaphore_signal(z_sem, inc=1, device_id=device, device_id_type=MESH)
    copies[3].wait()
    for copy in frame_copies:
        copy.wait()
    for j in range(2):
        cos = dot(frames[...], table[:, 256 * j : 256 * j + 256], ((1,), (0,)))
        sin = dot(frames[...], table[:, 512 + 256 * j : 768 + 256 * j], ((1,), (0,)))
        square = (cos * cos + sin * sin) * 0.25
        energy[:, 256 * j : 256 * j + 256] = square
        energy_t[256 * j : 256 * j + 256, :] = square.T
    for copy in w_copies:
        copy.wait()
    act_sibling.wait()
    act_pass.wait()
    pl.semaphore_wait(z_sem, 3)

    for t in range(ITERS):
        w_half = [
            jnp.concatenate([wb[2 * h].reshape(512, 128), wb[2 * h + 1].reshape(512, 128)], axis=1)
            for h in range(2)
        ]
        if t == 0:
            half = mass[0, 0] + mass[0, 1]
        else:
            half = jnp.concatenate(halves, axis=1)
        mass_half[t, 0] = half
        mass_copy = remote(mass_half.at[t, 0], mass_half.at[t, 1], mass_send.at[t], mass_recv.at[t], sibling)
        mass_copy.start()
        hb = [acts[f, here].astype(BF16) for f in range(4)]
        hb = [jnp.concatenate(hb[:2], axis=1), jnp.concatenate(hb[2:], axis=1)]
        rebuilt = dot(hb[0], w_half[0], ((1,), (1,))) + dot(hb[1], w_half[1], ((1,), (1,)))
        ratios = (energy[...] / rebuilt).astype(BF16)
        part_copies, own_part = [], []
        for h in range(2):
            own_part.append(dot(ratios, w_half[h], ((1,), (0,))))
            part[t, h] = own_part[h].astype(BF16)
            copy = remote(part.at[t, h], part_got.at[t, h], part_send.at[t, h], part_recv.at[t, h], sibling)
            copy.start()
            part_copies.append(copy)
        mass_copy.wait()
        inverse = 1.0 / (mass_half[t, 0] + mass_half[t, 1])
        hb = []
        for h in range(2):
            part_copies[h].wait()
            factor = (own_part[h] + part_got[t, h].astype(F32)) * inverse[:, 256 * h : 256 * h + 256]
            pieces = []
            for k in range(2):
                new = acts[2 * h + k, here] * factor[:, 128 * k : 128 * k + 128]
                acts[2 * h + k, here] = new
                pieces.append(new.astype(BF16))
            hb.append(jnp.concatenate(pieces, axis=1))
            tot[t, :, 256 * h : 256 * h + 256] = jnp.sum(hb[h].astype(F32), axis=0, keepdims=True)

        for slot in range(3):
            remote(tot.at[t], z_got.at[t, slot], z_sems.at[0, t], z_sems.at[1, t], z_peers[slot]).start()

        rebuilt = dot(w_half[0], hb[0], ((1,), (1,))) + dot(w_half[1], hb[1], ((1,), (1,)))
        ratios = (energy_t[...] / rebuilt).astype(BF16)
        for h in range(2):
            term = dot(ratios, hb[h], ((1,), (0,))).astype(BF16)
            for k in range(2):
                t_send[2 * h + k] = term[:, 128 * k : 128 * k + 128].reshape(32, 16, 128)
            for slot, (dx, dy, dz) in enumerate(OFFSETS):
                owner = 16 * y_his[dy] + 4 * zs[dz] + xs[dx]
                remote(
                    t_send.at[2 * h + y_los[dy], owner], t_got.at[h, slot],
                    t_sems.at[0, h], t_sems.at[1, h], chip(dx, dy, dz),
                ).start()
        for s in range(2):
            pltpu.make_async_copy(z_got.at[t], z_got.at[t], z_sems.at[s, t]).wait()
        plane = tot[t]
        for slot in range(3):
            plane = plane + z_got[t, slot]
        tot_z[t] = plane
        for slot, (dx, dy) in enumerate(PLANE):
            remote(
                tot_z.at[t], xy_got.at[t, slot], xy_sems.at[0, t], xy_sems.at[1, t], chip(dx, dy, 0)
            ).start()

        if t == ITERS - 1:
            final = remote(acts.at[far, here], acts.at[far, here], fin_sem.at[0], fin_sem.at[1], across)
            final.start()

        for h in range(2):
            summed = t_send[2 * h + y_lo, g].astype(F32)
            for s in range(2):
                pltpu.make_async_copy(t_got.at[h], t_got.at[h], t_sems.at[s, h]).wait()
            summed = summed + jnp.sum(t_got[h].astype(F32), axis=0)
            own_w[h] = own_w[h] * summed
            if t < ITERS - 1:
                mine = vb.at[2 * h + y_lo, g]
                peers = [chip(*offset) for offset in OFFSETS]
            else:
                mine = w_last.at[2 * h + y_lo, 4 * z + x]
                peers = [
                    (16 * (1 - y_lo if dy else y_lo) + 4 * zs[dz] + xs[dx], fr)
                    for dx, dy, dz in OFFSETS
                    if dy < 2
                ]
            mine[...] = own_w[h].astype(BF16)
            for device in peers:
                remote(mine, mine, t_sems.at[2, h], t_sems.at[3, h], device).start()
        if t == ITERS - 1:
            final.wait()
            a_copy = pltpu.make_async_copy(acts.at[fr], a_out, local_sem.at[1])
            a_copy.start()
        for s in range(2):
            pltpu.make_async_copy(xy_got.at[t], xy_got.at[t], xy_sems.at[s, t]).wait()
        inv_total = 1.0 / (tot_z[t] + jnp.sum(xy_got[t], axis=0))
        if t < ITERS - 1:
            for h in range(2):
                low = inv_total[:, 256 * h : 256 * h + 128]
                high = inv_total[:, 256 * h + 128 : 256 * h + 256]
                own_w[h] = own_w[h] * jnp.where(y_lo == 0, low, high)
        halves = []
        for h in range(2):
            arrived = t_got.at[h] if t < ITERS - 1 else t_got.at[h, pl.ds(0, 31)]
            for s in range(2, 4):
                pltpu.make_async_copy(arrived, arrived, t_sems.at[s, h]).wait()
            for q in (2 * h, 2 * h + 1):
                scale_q = inv_total[:, 128 * q : 128 * q + 128]
                if t < ITERS - 1:
                    block = vb[q].reshape(512, 128).astype(F32) * scale_q
                    halves.append(jnp.sum(block, axis=0, keepdims=True))
                    wb[q] = block.astype(BF16).reshape(32, 16, 128)
                else:
                    block = w_last[q].reshape(256, 128).astype(F32)
                    w_out[:, 128 * q : 128 * q + 128] = block * scale_q
        if t == ITERS - 1:
            a_copy.wait()


def shards(waveform, starts, templates, activations):
    hbm = pl.BlockSpec(memory_space=pltpu.HBM)
    vmem = pl.BlockSpec(memory_space=pltpu.VMEM)
    dma = pltpu.SemaphoreType.DMA
    scratch = [
        pltpu.SMEM((FR,), jnp.int32),
        pltpu.VMEM((16, 128), F32),
        pltpu.VMEM((272, 128), F32),
        pltpu.VMEM((FLEN, 1024), BF16),
        pltpu.VMEM((256, K), F32),
        pltpu.VMEM((4, 512, 128), F32),
        pltpu.VMEM((16 * FR // GROUPS, 128), F32),
        pltpu.VMEM((256, FLEN), BF16),
        pltpu.VMEM((256, 512), F32),
        pltpu.VMEM((512, 256), F32),
        pltpu.VMEM((4, 32, 16, 128), BF16),
        pltpu.VMEM((2, 16, 128), F32),
        pltpu.VMEM((4, 16, 16, 128), BF16),
        pltpu.VMEM((4, 32, 16, 128), BF16),
        pltpu.VMEM((ITERS, 2, 256, 256), BF16),
        pltpu.VMEM((ITERS, 2, 256, 256), BF16),
        pltpu.VMEM((4, 32, 16, 128), BF16),
        pltpu.VMEM((2, 63, 16, 128), BF16),
        pltpu.VMEM((ITERS, 1, K), F32),
        pltpu.VMEM((ITERS, 1, K), F32),
        pltpu.VMEM((ITERS, 3, 1, K), F32),
        pltpu.VMEM((ITERS, 15, 1, K), F32),
        pltpu.VMEM((1, 2, 1, K), F32),
        pltpu.VMEM((ITERS, 2, 1, K), F32),
        dma((6,)),
        dma((2,)),
        dma((GROUPS,)),
        dma((GROUPS,)),
        dma((3,)),
        dma((3,)),
        dma((5,)),
        dma((5,)),
        dma((ITERS, 2)),
        dma((ITERS, 2)),
        dma((4, 2)),
        dma((2, ITERS)),
        dma((2, ITERS)),
        dma((ITERS,)),
        dma((ITERS,)),
        dma((2,)),
        pltpu.SemaphoreType.REGULAR,
        pltpu.SemaphoreType.REGULAR,
    ]
    return pl.pallas_call(
        kernel,
        out_shape=(
            jax.ShapeDtypeStruct((256, K), F32),
            jax.ShapeDtypeStruct((512, 128), F32),
        ),
        in_specs=[hbm] * 6,
        out_specs=(vmem, hbm),
        scratch_shapes=scratch,
        compiler_params=pltpu.CompilerParams(
            collective_id=0, has_side_effects=True, vmem_limit_bytes=60 * 2**20
        ),
    )(
        waveform.reshape(256, 128),
        starts,
        jnp.asarray(hann_window()),
        jnp.asarray(half_tables()),
        templates,
        activations,
    )


def solution(mesh):
    in_specs = (P(("tm", "freq")), P(("tm", "freq")), P("freq", None), P("tm", "freq"))
    out_specs = (P("freq", None), P("tm", "freq"))
    return jax.shard_map(shards, mesh=mesh, in_specs=in_specs, out_specs=out_specs, check_vma=False)
```

```python
import jax
import jax.numpy as jnp
import numpy as np
from jax import lax
from jax.experimental import pallas as pl
from jax.experimental.pallas import tpu as pltpu
from jax.sharding import PartitionSpec as P

FLEN = 2048
BINS = 1024
K = 512
ITERS = 2
SEG = 32768
FR = 128
GROUPS = 4
MESH = pl.DeviceIdType.MESH
F32 = jnp.float32
BF16 = jnp.bfloat16


def half_tables():
    row = np.arange(FLEN, dtype=np.int64)[:, None]
    tables = []
    for core in range(2):
        bins = np.concatenate([np.arange(256) + 256 * core, np.arange(256) + 512 + 256 * core])
        phase = ((row * bins[None, :]) % FLEN).astype(np.float32) * np.float32(2.0 * np.pi / FLEN)
        tables.append(np.concatenate([np.cos(phase), -np.sin(phase)], axis=1))
    return np.stack(tables).astype(jnp.bfloat16)


def hann_window():
    steps = np.arange(FLEN, dtype=np.float32) * np.float32(2.0 * np.pi / FLEN)
    return (np.float32(0.5) - np.float32(0.5) * np.cos(steps)).reshape(16, 128)


def hops(offset):
    return sum(min(v, 4 - v) for v in offset)


OFFSETS = sorted(
    [(dx, dy, dz) for dz in range(4) for dy in range(4) for dx in range(4) if dx or dy or dz],
    key=lambda offset: -hops(offset),
)


PLANE = sorted(
    [(dx, dy) for dy in range(4) for dx in range(4) if dx or dy],
    key=lambda offset: -hops(offset),
)


def dot(a, b, dims):
    return lax.dot_general(a, b, (dims, ((), ())), preferred_element_type=F32)


def kernel(
    wave_hbm, starts_hbm, window_hbm, table_hbm, templ_hbm, act_hbm, w_out, a_out,
    starts, window, wave, table, templ, acts, gathered, frames, energy, energy_t, wb, own_w, w_last,
    vb, part, part_got, t_send, t_got, tot, tot_z, z_got, xy_got, mass, mass_half,
    local_sem, rim_sem, frame_send, frame_recv, act_send, act_recv, w_send, w_recv,
    part_send, part_recv, t_sems, z_sems, xy_sems, mass_send, mass_recv, fin_sem, y_sem, z_sem,
):
    tm = lax.axis_index("tm")
    fr = lax.axis_index("freq")
    x, z, y_lo = lax.rem(tm, 4), lax.rem(lax.div(tm, 4), 4), lax.div(tm, 16)
    y_hi, core = lax.div(fr, 2), lax.rem(fr, 2)
    y = 2 * y_hi + y_lo
    xs = [lax.rem(x + d, 4) for d in range(4)]
    zs = [lax.rem(z + d, 4) for d in range(4)]
    ys = [lax.rem(y + d, 4) for d in range(4)]
    y_los = [lax.rem(v, 2) for v in ys]
    y_his = [lax.div(v, 2) for v in ys]

    def chip(dx, dy, dz):
        return (y_los[dy] * 16 + zs[dz] * 4 + xs[dx], y_his[dy] * 2 + core)

    def remote(src, dst, send, recv, device):
        return pltpu.make_async_remote_copy(
            src_ref=src, dst_ref=dst, send_sem=send, recv_sem=recv,
            device_id=device, device_id_type=MESH,
        )

    sibling = (tm, 2 * y_hi + 1 - core)
    across = (tm, 2 * (1 - y_hi) + core)
    beside = (lax.rem(tm + 16, 32), 2 * (1 - y_hi) + core)
    place = 4 * tm + fr
    following = lax.rem(place + 1, 128)
    previous = lax.rem(place + 127, 128)
    following = (lax.div(following, 4), lax.rem(following, 4))
    previous = (lax.div(previous, 4), lax.rem(previous, 4))

    copies = [
        pltpu.make_async_copy(wave_hbm, wave.at[pl.ds(0, 256)], local_sem.at[0]),
        pltpu.make_async_copy(act_hbm, acts.at[fr], local_sem.at[1]),
        pltpu.make_async_copy(templ_hbm, templ, local_sem.at[2]),
        pltpu.make_async_copy(table_hbm.at[core], table, local_sem.at[3]),
        pltpu.make_async_copy(starts_hbm, starts, local_sem.at[4]),
        pltpu.make_async_copy(window_hbm, window, local_sem.at[5]),
    ]
    barrier = pltpu.get_barrier_semaphore()
    axis_peers = [chip(d, 0, 0) for d in (1, 2, 3)]
    y_peers = [chip(0, d, 0) for d in (1, 2, 3)]
    z_peers = [chip(0, 0, d) for d in (1, 2, 3)]
    for device in [following, sibling] + axis_peers + y_peers + z_peers:
        pl.semaphore_signal(barrier, inc=1, device_id=device, device_id_type=MESH)
    for copy in copies:
        copy.start()
    copies[2].wait()
    for h in range(4):
        wb[h, pl.ds(16 * y_hi, 16)] = templ[:, 128 * h : 128 * h + 128].astype(BF16).reshape(16, 16, 128)
    mass[0, pl.ds(y_hi, 1)] = jnp.sum(templ[...], axis=0, keepdims=True).reshape(1, 1, K)
    g = 16 * y_hi + 4 * z + x
    for h in range(2):

        @pl.when(y_lo == h)
        def _():
            rows = pl.ds(pl.multiple_of(16 * (4 * z + x), 16), 16)
            for k in range(2):
                own_w[k] = templ[rows, 256 * k + 128 * h : 256 * k + 128 * h + 128]

    copies[0].wait()
    copies[1].wait()
    pl.semaphore_wait(barrier, 11)

    rim = remote(wave.at[pl.ds(0, 16)], wave.at[pl.ds(256, 16)], rim_sem.at[0], rim_sem.at[1], previous)
    rim.start()
    here = pl.ds(pl.multiple_of(256 * y_hi, 256), 256)
    there = pl.ds(pl.multiple_of(256 * (1 - y_hi), 256), 256)
    act_across = remote(acts.at[fr, there], acts.at[fr, there], act_send.at[0], act_recv.at[0], across)
    act_across.start()
    act_sibling = remote(acts.at[fr, here], acts.at[fr, here], act_send.at[1], act_recv.at[1], sibling)
    act_sibling.start()
    w_copies = []
    for h in range(4):
        rows = wb.at[h, pl.ds(16 * y_hi, 16)]
        w_copies.append(remote(rows, rows, w_send.at[h], w_recv.at[h], beside))
    w_copies.append(remote(mass.at[0, y_hi], mass.at[0, y_hi], w_send.at[4], w_recv.at[4], beside))
    for copy in w_copies:
        copy.start()
    for device in y_peers:
        pl.semaphore_signal(y_sem, inc=1, device_id=device, device_id_type=MESH)

    rim.wait()
    copies[4].wait()
    copies[5].wait()

    @pl.when(place == 127)
    def _():
        wave[pl.ds(256, 16)] = jnp.zeros((16, 128), F32)

    lanes = lax.broadcasted_iota(jnp.int32, (16, 128), 1)
    scale = window[...]
    size = FR // GROUPS
    frame_copies = []
    for group in range(GROUPS):

        def gather(i, carry):
            start = lax.rem(starts[group * size + i], SEG)
            row, shift = lax.div(start, 128), lax.rem(start, 128)
            low = wave[pl.ds(row, 16), :]
            high = wave[pl.ds(row + 1, 16), :]
            joined = jnp.where(lanes >= shift, low, high)
            rolled = pltpu.roll(joined, lax.rem(128 - shift, 128), 1)
            gathered[pl.ds(i, 16, stride=size), :] = rolled * scale
            return carry

        lax.fori_loop(0, size, gather, 0, unroll=8)
        rows = pl.ds(pl.multiple_of(FR * core + group * size, size), size)
        for i in range(16):
            frames[rows, 128 * i : 128 * i + 128] = gathered[size * i : size * i + size, :].astype(BF16)
        copy = remote(frames.at[rows], frames.at[rows], frame_send.at[group], frame_recv.at[group], sibling)
        copy.start()
        frame_copies.append(copy)

    act_across.wait()
    far = 2 * (1 - y_hi) + core
    act_pass = remote(acts.at[far, here], acts.at[far, here], act_send.at[2], act_recv.at[2], sibling)
    act_pass.start()
    pl.semaphore_wait(y_sem, 3)
    for device in z_peers:
        pl.semaphore_signal(z_sem, inc=1, device_id=device, device_id_type=MESH)
    copies[3].wait()
    for copy in frame_copies:
        copy.wait()
    for j in range(2):
        cos = dot(frames[...], table[:, 256 * j : 256 * j + 256], ((1,), (0,)))
        sin = dot(frames[...], table[:, 512 + 256 * j : 768 + 256 * j], ((1,), (0,)))
        square = (cos * cos + sin * sin) * 0.25
        energy[:, 256 * j : 256 * j + 256] = square
        energy_t[256 * j : 256 * j + 256, :] = square.T
    for copy in w_copies:
        copy.wait()
    act_sibling.wait()
    act_pass.wait()
    pl.semaphore_wait(z_sem, 3)

    for t in range(ITERS):
        w_half = [
            jnp.concatenate([wb[2 * h].reshape(512, 128), wb[2 * h + 1].reshape(512, 128)], axis=1)
            for h in range(2)
        ]
        if t == 0:
            half = mass[0, 0] + mass[0, 1]
        else:
            half = jnp.concatenate(halves, axis=1)
        mass_half[t, 0] = half
        mass_copy = remote(mass_half.at[t, 0], mass_half.at[t, 1], mass_send.at[t], mass_recv.at[t], sibling)
        mass_copy.start()
        hb = [acts[f, here].astype(BF16) for f in range(4)]
        hb = [jnp.concatenate(hb[:2], axis=1), jnp.concatenate(hb[2:], axis=1)]
        rebuilt = dot(hb[0], w_half[0], ((1,), (1,))) + dot(hb[1], w_half[1], ((1,), (1,)))
        ratios = (energy[...] / rebuilt).astype(BF16)
        part_copies, own_part = [], []
        for h in range(2):
            own_part.append(dot(ratios, w_half[h], ((1,), (0,))))
            part[t, h] = own_part[h].astype(BF16)
            copy = remote(part.at[t, h], part_got.at[t, h], part_send.at[t, h], part_recv.at[t, h], sibling)
            copy.start()
            part_copies.append(copy)
        mass_copy.wait()
        inverse = 1.0 / (mass_half[t, 0] + mass_half[t, 1])
        hb = []
        for h in range(2):
            part_copies[h].wait()
            factor = (own_part[h] + part_got[t, h].astype(F32)) * inverse[:, 256 * h : 256 * h + 256]
            pieces = []
            for k in range(2):
                new = acts[2 * h + k, here] * factor[:, 128 * k : 128 * k + 128]
                acts[2 * h + k, here] = new
                pieces.append(new.astype(BF16))
            hb.append(jnp.concatenate(pieces, axis=1))
            tot[t, :, 256 * h : 256 * h + 256] = jnp.sum(hb[h].astype(F32), axis=0, keepdims=True)

        for slot in range(3):
            remote(tot.at[t], z_got.at[t, slot], z_sems.at[0, t], z_sems.at[1, t], z_peers[slot]).start()

        rebuilt = dot(w_half[0], hb[0], ((1,), (1,))) + dot(w_half[1], hb[1], ((1,), (1,)))
        ratios = (energy_t[...] / rebuilt).astype(BF16)
        for h in range(2):
            term = dot(ratios, hb[h], ((1,), (0,))).astype(BF16)
            for k in range(2):
                t_send[2 * h + k] = term[:, 128 * k : 128 * k + 128].reshape(32, 16, 128)
            for slot, (dx, dy, dz) in enumerate(OFFSETS):
                owner = 16 * y_his[dy] + 4 * zs[dz] + xs[dx]
                remote(
                    t_send.at[2 * h + y_los[dy], owner], t_got.at[h, slot],
                    t_sems.at[0, h], t_sems.at[1, h], chip(dx, dy, dz),
                ).start()
        if t == ITERS - 1:
            final = remote(acts.at[far, here], acts.at[far, here], fin_sem.at[0], fin_sem.at[1], across)
            final.start()

        for h in range(2):
            summed = t_send[2 * h + y_lo, g].astype(F32)
            for s in range(2):
                pltpu.make_async_copy(t_got.at[h], t_got.at[h], t_sems.at[s, h]).wait()
            summed = summed + jnp.sum(t_got[h].astype(F32), axis=0)
            own_w[h] = own_w[h] * summed
            if t < ITERS - 1:
                mine = vb.at[2 * h + y_lo, g]
                peers = [chip(*offset) for offset in OFFSETS]
            else:
                mine = w_last.at[2 * h + y_lo, 4 * z + x]
                peers = [
                    (16 * (1 - y_lo if dy else y_lo) + 4 * zs[dz] + xs[dx], fr)
                    for dx, dy, dz in OFFSETS
                    if dy < 2
                ]
            mine[...] = own_w[h].astype(BF16)
            for device in peers:
                remote(mine, mine, t_sems.at[2, h], t_sems.at[3, h], device).start()
            if h == 0:
                for s in range(2):
                    pltpu.make_async_copy(z_got.at[t], z_got.at[t], z_sems.at[s, t]).wait()
                plane = tot[t]
                for slot in range(3):
                    plane = plane + z_got[t, slot]
                tot_z[t] = plane
                for slot, (dx, dy) in enumerate(PLANE):
                    remote(
                        tot_z.at[t], xy_got.at[t, slot], xy_sems.at[0, t], xy_sems.at[1, t], chip(dx, dy, 0)
                    ).start()
        if t == ITERS - 1:
            final.wait()
            a_copy = pltpu.make_async_copy(acts.at[fr], a_out, local_sem.at[1])
            a_copy.start()
        for s in range(2):
            pltpu.make_async_copy(xy_got.at[t], xy_got.at[t], xy_sems.at[s, t]).wait()
        inv_total = 1.0 / (tot_z[t] + jnp.sum(xy_got[t], axis=0))
        if t < ITERS - 1:
            for h in range(2):
                low = inv_total[:, 256 * h : 256 * h + 128]
                high = inv_total[:, 256 * h + 128 : 256 * h + 256]
                own_w[h] = own_w[h] * jnp.where(y_lo == 0, low, high)
        halves = []
        for h in range(2):
            arrived = t_got.at[h] if t < ITERS - 1 else t_got.at[h, pl.ds(0, 31)]
            for s in range(2, 4):
                pltpu.make_async_copy(arrived, arrived, t_sems.at[s, h]).wait()
            for q in (2 * h, 2 * h + 1):
                scale_q = inv_total[:, 128 * q : 128 * q + 128]
                if t < ITERS - 1:
                    block = vb[q].reshape(512, 128).astype(F32) * scale_q
                    halves.append(jnp.sum(block, axis=0, keepdims=True))
                    wb[q] = block.astype(BF16).reshape(32, 16, 128)
                else:
                    block = w_last[q].reshape(256, 128).astype(F32)
                    w_out[:, 128 * q : 128 * q + 128] = block * scale_q
        if t == ITERS - 1:
            a_copy.wait()


def shards(waveform, starts, templates, activations):
    hbm = pl.BlockSpec(memory_space=pltpu.HBM)
    vmem = pl.BlockSpec(memory_space=pltpu.VMEM)
    dma = pltpu.SemaphoreType.DMA
    scratch = [
        pltpu.SMEM((FR,), jnp.int32),
        pltpu.VMEM((16, 128), F32),
        pltpu.VMEM((272, 128), F32),
        pltpu.VMEM((FLEN, 1024), BF16),
        pltpu.VMEM((256, K), F32),
        pltpu.VMEM((4, 512, 128), F32),
        pltpu.VMEM((16 * FR // GROUPS, 128), F32),
        pltpu.VMEM((256, FLEN), BF16),
        pltpu.VMEM((256, 512), F32),
        pltpu.VMEM((512, 256), F32),
        pltpu.VMEM((4, 32, 16, 128), BF16),
        pltpu.VMEM((2, 16, 128), F32),
        pltpu.VMEM((4, 16, 16, 128), BF16),
        pltpu.VMEM((4, 32, 16, 128), BF16),
        pltpu.VMEM((ITERS, 2, 256, 256), BF16),
        pltpu.VMEM((ITERS, 2, 256, 256), BF16),
        pltpu.VMEM((4, 32, 16, 128), BF16),
        pltpu.VMEM((2, 63, 16, 128), BF16),
        pltpu.VMEM((ITERS, 1, K), F32),
        pltpu.VMEM((ITERS, 1, K), F32),
        pltpu.VMEM((ITERS, 3, 1, K), F32),
        pltpu.VMEM((ITERS, 15, 1, K), F32),
        pltpu.VMEM((1, 2, 1, K), F32),
        pltpu.VMEM((ITERS, 2, 1, K), F32),
        dma((6,)),
        dma((2,)),
        dma((GROUPS,)),
        dma((GROUPS,)),
        dma((3,)),
        dma((3,)),
        dma((5,)),
        dma((5,)),
        dma((ITERS, 2)),
        dma((ITERS, 2)),
        dma((4, 2)),
        dma((2, ITERS)),
        dma((2, ITERS)),
        dma((ITERS,)),
        dma((ITERS,)),
        dma((2,)),
        pltpu.SemaphoreType.REGULAR,
        pltpu.SemaphoreType.REGULAR,
    ]
    return pl.pallas_call(
        kernel,
        out_shape=(
            jax.ShapeDtypeStruct((256, K), F32),
            jax.ShapeDtypeStruct((512, 128), F32),
        ),
        in_specs=[hbm] * 6,
        out_specs=(vmem, hbm),
        scratch_shapes=scratch,
        compiler_params=pltpu.CompilerParams(
            collective_id=0, has_side_effects=True, vmem_limit_bytes=60 * 2**20
        ),
    )(
        waveform.reshape(256, 128),
        starts,
        jnp.asarray(hann_window()),
        jnp.asarray(half_tables()),
        templates,
        activations,
    )


def solution(mesh):
    in_specs = (P(("tm", "freq")), P(("tm", "freq")), P("freq", None), P("tm", "freq"))
    out_specs = (P("freq", None), P("tm", "freq"))
    return jax.shard_map(shards, mesh=mesh, in_specs=in_specs, out_specs=out_specs, check_vma=False)
```
